512 devices in a mesh: dp: 4 (over y_lo, core), pipe: 16 (over z), tensor: 8 (over y_hi, x).
Axes of the slice: x: 4, y: 4 (y_hi: 2, y_lo: 2; y = y_hi * 2 + y_lo), z: 16, core: 2. Of those that a mesh axis runs over, the one named last changes fastest.
Arguments:
- inputs: bfloat16 [16, 4, 256, 8192], P('pipe', 'dp', None, 'tensor'), may hold values from -64 to 64
- norm_gain: float32 [16, 8192], P('pipe', 'tensor'), may hold values from 0.1 to 1.9
- queries: bfloat16 [16, 4, 256, 8192], P('pipe', 'dp', None, 'tensor'), may hold values from -8 to 8
- saved_keys: bfloat16 [16, 4, 256, 1024], P('pipe', 'dp', None, 'tensor'), may hold values from -8 to 8
- saved_values: bfloat16 [16, 4, 256, 1024], P('pipe', 'dp', None, 'tensor'), may hold values from -6 to 6
- attn_out_grad: bfloat16 [16, 4, 256, 8192], P('pipe', 'dp', None, 'tensor'), may hold values from -6 to 6
- kv_projection: bfloat16 [16, 2048, 8192], P('pipe', 'dp', 'tensor'), may hold values from -1 to 1
- top_grad: bfloat16 [4, 256, 8192], P('dp', None, 'tensor'), may hold values from -3 to 3
- doc_lengths: int32 [4, 4], P('dp'), may hold values from 1 to 128, 256 in all within a row
Outputs:
- section_grads: bfloat16 [16, 4, 256, 8192], P('pipe', 'dp', None, 'tensor')
- kv_projection_grad: bfloat16 [16, 2048, 8192], P('pipe', 'dp', 'tensor')
- norm_gain_grad: float32 [16, 8192], P('pipe', 'tensor')
The draws below stay inside these ranges and needn't reach their ends.
Inputs may be any that keep to these rules, and one draw needn't show every extreme that they name: `doc_lengths`: each row sums to 256.
All inputs are finite; a program needn't handle non-finite values.
Results may differ from the reference program's by a relative error of at most 0.015.
Values may be sent and summed in bfloat16 or wider, within the bound.
No kernel may reach another device: no remote copies, remote signals or barrier semaphores. Data moves between devices by JAX's collectives and lax.ppermute only.
A program may use at most 128 MiB of HBM per device.

```python
import math
import jax
import jax.numpy as jnp
import numpy as np
from jax import lax

D = 8192
H = 64
KVH = 8
HD = 128
SEQ = 256
NDOC = 4
SECTIONS = 16
SEQS = 4
KVW = 2048


def common_direction(key):
    shared_key = jax.random.fold_in(key, 31)
    dir_key, region_key = jax.random.split(shared_key, 2)
    direction = jnp.clip(jax.random.normal(dir_key, (SECTIONS, D)), -3.0, 3.0)
    region_coef = jax.random.uniform(region_key, (SECTIONS, 16), minval=-0.5, maxval=1.5)
    region_of = jnp.arange(D) * 16 // D
    weights = region_coef[:, region_of]
    return (direction, weights)


def draw_inputs(key, part):
    common_key = key
    key = jax.random.fold_in(key, 5)
    base_key, row_key, col_key = jax.random.split(key, 3)
    direction, weights = common_direction(common_key)
    base = jnp.clip(jax.random.normal(base_key, (SECTIONS, SEQS, SEQ, D)), -4.0, 4.0)
    row_scale = jnp.exp(jax.random.uniform(row_key, (SECTIONS, SEQS, SEQ, 1), minval=jnp.log(0.3), maxval=jnp.log(3.0)))
    aligned = base + 2.0 * (weights * direction)[:, None, None, :]
    ramp = 3.0 ** (jnp.arange(D, dtype=jnp.float32) / D)
    column_scale_factor = ramp * jnp.exp(jax.random.uniform(col_key, (D,), minval=-0.5, maxval=0.5))
    return jnp.clip(aligned * row_scale * column_scale_factor, -64.0, 64.0).astype(jnp.bfloat16)


def draw_kv_projection(key, part):
    common_key = key
    key = jax.random.fold_in(key, 11)
    noise_key, coef_key = jax.random.split(key, 2)
    direction, weights = common_direction(common_key)
    noise = jnp.clip(jax.random.normal(noise_key, (SECTIONS, KVW, D)), -4.0, 4.0)
    row_coef = jnp.clip(jax.random.normal(coef_key, (SECTIONS, KVW, 1)), -4.0, 4.0)
    mixed = (noise + row_coef * direction[:, None, :]) * (2.0 * D) ** (-0.5)
    return jnp.clip(mixed, -1.0, 1.0).astype(jnp.bfloat16)


def draw_queries(key, part):
    key = jax.random.fold_in(key, 7)
    base = jnp.clip(jax.random.normal(key, (SECTIONS, SEQS, SEQ, H * HD)), -4.0, 4.0)
    return base.astype(jnp.bfloat16)


def draw_saved_keys(key, part):
    key = jax.random.fold_in(key, 9)
    base = jnp.clip(jax.random.normal(key, (SECTIONS, SEQS, SEQ, KVH * HD)), -4.0, 4.0)
    return base.astype(jnp.bfloat16)


def level_of(rng, extent, pieces, least, top_value):
    gain = 1.0
    for position, shards_of in pieces:
        heights = jax.random.uniform(jax.random.fold_in(jax.random.fold_in(rng, 6), position), (shards_of,), jnp.float32, least / len(pieces), top_value / len(pieces))
        gain = gain * jnp.repeat(jnp.exp(heights), extent[position] // shards_of).reshape((-1,) + (1,) * (len(extent) - 1 - position))
    return gain


def length_profile(amount, total, reach, skew):
    weights = [(1 << 20) // math.isqrt(standing ** skew) + 1 for standing in range(2, amount + 1)]
    rest, counts = total - reach - (amount - 1), [1] * (amount - 1)
    while rest > 0:
        candidates = [i for i in range(amount - 1) if counts[i] < reach]
        pool, remaining = sum([weights[i] for i in candidates]), rest
        for i in candidates:
            addition = min(reach - counts[i], max(1, remaining * weights[i] // pool), rest)
            counts[i] = counts[i] + addition
            rest = rest - addition
    return np.array([reach] + counts)


def uneven(own_key, count, total, reach, skew):
    if count == 2:
        one = jax.random.randint(own_key, (), max(1, total - reach), min(reach, total - 1) + 1)
        return jnp.stack([one, total - one])
    sizes = jnp.asarray(length_profile(count, total, reach, skew), jnp.int32)
    couples = (count - 1) // 2
    giver, sink = sizes[1:1 + 2 * couples:2], sizes[2:2 + 2 * couples:2]
    slack = jnp.minimum(giver - 1, reach - sink)
    shifted = jax.random.randint(jax.random.fold_in(own_key, 1), (couples,), 0, 1 << 20) % (slack + 1)
    sizes = sizes.at[1:1 + 2 * couples:2].set(giver - shifted).at[2:2 + 2 * couples:2].set(sink + shifted)
    return sizes[jax.random.permutation(jax.random.fold_in(own_key, 2), count)]


def bell_draw(key, dims, scale, most, cuts=(), kind=jnp.bfloat16):
    entries = jax.random.normal(key, dims, jnp.float32) * scale
    if len(cuts) > 0:
        entries = level_of(key, dims, cuts, -0.22, 0.18) * entries
    return jnp.clip(entries, min=-most, max=most).astype(kind)


def setup_inputs(seed: int = 0) -> dict:
    seeds = jax.random.split(jax.random.key(seed), 10)
    return {
        "inputs": draw_inputs(jax.random.fold_in(seeds[9], 71), 0),
        "norm_gain": jnp.clip(1.0 + 0.18 * jax.random.normal(seeds[1], (SECTIONS, D), jnp.float32), 0.1, 1.9),
        "queries": draw_queries(jax.random.fold_in(seeds[9], 71), 0),
        "saved_keys": draw_saved_keys(jax.random.fold_in(seeds[9], 71), 0),
        "saved_values": bell_draw(seeds[4], (SECTIONS, SEQS, SEQ, KVH * HD), 1.0, 6.0, ((0, 16), (1, 4), (3, 8))),
        "attn_out_grad": bell_draw(seeds[5], (SECTIONS, SEQS, SEQ, H * HD), 1.0, 6.0, ((0, 16), (1, 4), (3, 8))),
        "kv_projection": draw_kv_projection(jax.random.fold_in(seeds[9], 71), 0),
        "top_grad": bell_draw(seeds[7], (SEQS, SEQ, D), 0.5, 3.0, ((0, 4), (2, 8))),
        "doc_lengths": jax.vmap(lambda own: uneven(own, NDOC, SEQ, SEQ // 2, 2))(jax.random.split(seeds[8], SEQS)).reshape((SEQS, NDOC)).astype(jnp.int32),
    }


EPSILON = 1e-05

def rounded_values(tensor):
    return lax.optimization_barrier(tensor.astype(jnp.bfloat16)).astype(jnp.float32)

def doc_mask(lengths):
    bounds = jnp.cumsum(lengths.astype(jnp.int32))
    places = jnp.arange(SEQ, dtype=jnp.int32)
    owner = lax.optimization_barrier(jnp.sum((places[:, None] >= bounds[None, :]).astype(jnp.int32), axis=1))
    return (owner[:, None] == owner[None, :]) & (places[:, None] >= places[None, :])

def attention_back(query, key_rows, value_rows, out_grad, allowed):
    kv_heads = key_rows.shape[-1] // HD
    group = H // KVH
    query_heads = query.astype(jnp.float32).reshape(-1, kv_heads, group, HD)
    key_heads = key_rows.astype(jnp.float32).reshape(-1, kv_heads, HD)
    value_heads = value_rows.astype(jnp.float32).reshape(-1, kv_heads, HD)
    grad_heads = out_grad.astype(jnp.float32).reshape(-1, kv_heads, group, HD)
    factor = HD ** (-0.5)
    scores = jnp.einsum('ikgd,jkd->kgij', query_heads, key_heads) * factor
    scores = jnp.where(allowed, scores, -1e+30)
    row_max = lax.optimization_barrier(jnp.max(scores, axis=-1, keepdims=True))
    expos = jnp.where(allowed, jnp.exp(scores - row_max), 0.0)
    probs = expos / lax.optimization_barrier(jnp.sum(expos, axis=-1, keepdims=True))
    probs_b = rounded_values(probs)
    grad_values = jnp.einsum('kgij,ikgd->jkd', probs_b, grad_heads).astype(jnp.bfloat16)
    grad_probs = jnp.einsum('ikgd,jkd->kgij', grad_heads, value_heads)
    centre = lax.optimization_barrier(jnp.sum(probs * grad_probs, axis=-1, keepdims=True))
    grad_scores = rounded_values(probs * (grad_probs - centre) * factor)
    grad_keys = jnp.einsum('kgij,ikgd->jkd', grad_scores, query_heads).astype(jnp.bfloat16)
    return jnp.stack([grad_keys, grad_values], axis=2).reshape(-1, kv_heads * 2 * HD)

def reference(inputs, norm_gain, queries, saved_keys, saved_values, attn_out_grad, kv_projection, top_grad, doc_lengths):
    masks = jax.vmap(doc_mask)(doc_lengths)
    gradient_scale_factor = (SEQS * SEQ) ** (-0.5)

    def one_section(section_data):
        section_in, gain_row, query_s, keys_s, values_s, dout_s, proj_s = section_data
        wide = section_in.astype(jnp.float32)
        row_rms = jnp.sqrt(lax.optimization_barrier(jnp.mean(wide * wide, axis=-1, keepdims=True)) + EPSILON)
        unit_rows = wide / row_rms
        rms_scaled_rows = (unit_rows * gain_row).astype(jnp.bfloat16)
        gradient_key_value = jax.vmap(attention_back)(query_s, keys_s, values_s, dout_s, masks)
        grad_normed = jnp.einsum('bsk,kd->bsd', gradient_key_value.astype(jnp.float32), proj_s.astype(jnp.float32))
        scaled = grad_normed * gain_row
        mean_prod = lax.optimization_barrier(jnp.mean(scaled * unit_rows, axis=-1, keepdims=True))
        contrib = (scaled - unit_rows * mean_prod) / row_rms
        gain_grad = lax.optimization_barrier(jnp.sum(grad_normed * unit_rows, axis=(0, 1))) * gradient_scale_factor
        running_partial_totals = rounded_values(jnp.einsum('cqa,cqo->cao', gradient_key_value.astype(jnp.float32), rms_scaled_rows.astype(jnp.float32)) * gradient_scale_factor)
        return (contrib, gain_grad, lax.optimization_barrier(jnp.sum(running_partial_totals, axis=0)))
    contribs, gain_grads, weight_grads = lax.map(one_section, (inputs, norm_gain, queries, saved_keys, saved_values, attn_out_grad, kv_projection))
    suffix = jnp.flip(jnp.cumsum(jnp.flip(contribs, 0), axis=0), 0)
    section_grads = (top_grad.astype(jnp.float32)[None] + suffix).astype(jnp.bfloat16)
    return (section_grads, weight_grads.astype(jnp.bfloat16), gain_grads)
```

```python
import jax
import jax.numpy as jnp
from jax import lax
from jax.sharding import PartitionSpec as P

D = 8192
H = 64
KVH = 8
HD = 128
EPSILON = 1e-05


def doc_mask(lengths, sequence_length):
    bounds = jnp.cumsum(lengths)
    places = jnp.arange(sequence_length, dtype=jnp.int32)
    owner = jnp.sum((places[:, None] >= bounds[None, :]).astype(jnp.int32), axis=1)
    return (owner[:, None] == owner[None, :]) & (places[:, None] >= places[None, :])


def attention_back(query, key_rows, value_rows, out_grad, allowed):
    kv_heads = key_rows.shape[-1] // HD
    group = H // KVH
    sequence_length = query.shape[0]
    query_heads = query.reshape(sequence_length, kv_heads, group, HD)
    key_heads = key_rows.reshape(sequence_length, kv_heads, HD)
    value_heads = value_rows.reshape(sequence_length, kv_heads, HD)
    grad_heads = out_grad.reshape(sequence_length, kv_heads, group, HD)
    factor = HD ** (-0.5)
    scores = (
        jnp.einsum("ikgd,jkd->kgij", query_heads, key_heads, preferred_element_type=jnp.float32)
        * factor
    )
    scores = jnp.where(allowed, scores, -1e30)
    row_max = jnp.max(scores, axis=-1, keepdims=True)
    expos = jnp.where(allowed, jnp.exp(scores - row_max), 0.0)
    probs = expos / jnp.sum(expos, axis=-1, keepdims=True)
    probs_b = probs.astype(jnp.bfloat16)
    grad_values = jnp.einsum(
        "kgij,ikgd->jkd", probs_b, grad_heads, preferred_element_type=jnp.float32
    ).astype(jnp.bfloat16)
    grad_probs = jnp.einsum(
        "ikgd,jkd->kgij", grad_heads, value_heads, preferred_element_type=jnp.float32
    )
    centre = jnp.sum(probs * grad_probs, axis=-1, keepdims=True)
    grad_scores = (probs * (grad_probs - centre) * factor).astype(jnp.bfloat16)
    grad_keys = jnp.einsum(
        "kgij,ikgd->jkd", grad_scores, query_heads, preferred_element_type=jnp.float32
    ).astype(jnp.bfloat16)
    return jnp.stack([grad_keys, grad_values], axis=2).reshape(sequence_length, kv_heads * 2 * HD)


def sum_over(vector, axis):
    count = lax.axis_size(axis)
    copies = jnp.broadcast_to(vector.reshape(1, -1, 128), (count, vector.size // 128, 128))
    return jnp.sum(lax.all_to_all(copies, axis, 0, 0), axis=0).reshape(vector.shape)


def body(
    inputs,
    norm_gain,
    queries,
    saved_keys,
    saved_values,
    attn_out_grad,
    kv_projection,
    top_grad,
    doc_lengths,
):
    tensor, sections = lax.axis_size("tensor"), lax.axis_size("pipe")
    projection = lax.all_gather(kv_projection[0], "dp", axis=0, tiled=True)
    wide = inputs[0, 0].astype(jnp.float32)
    gain_row = norm_gain[0]
    tokens, width = wide.shape
    row_sums = sum_over(jnp.sum(wide * wide, axis=1), "tensor")
    row_rms = jnp.sqrt(row_sums / D + EPSILON)[:, None]
    unit_rows = wide / row_rms
    normed = (unit_rows * gain_row).astype(jnp.bfloat16)
    allowed = doc_mask(doc_lengths[0], tokens)
    local_kv = attention_back(
        queries[0, 0], saved_keys[0, 0], saved_values[0, 0], attn_out_grad[0, 0], allowed
    )
    copies = jnp.broadcast_to(local_kv[None], (tensor,) + local_kv.shape)
    grad_kv = lax.all_to_all(copies, "tensor", 0, 0)
    columns = jnp.concatenate([grad_kv[head] for head in range(tensor)], axis=1)
    grad_normed = jnp.dot(columns, projection, preferred_element_type=jnp.float32)
    scaled = grad_normed * gain_row
    row_prods = sum_over(jnp.sum(scaled * unit_rows, axis=1), "tensor")
    contrib = ((scaled - unit_rows * (row_prods / D)[:, None]) / row_rms).astype(jnp.bfloat16)
    scale = (lax.axis_size("dp") * tokens) ** (-0.5)
    parts = lax.all_to_all(contrib.reshape(sections, tokens // sections, width), "pipe", 0, 0)
    gain_grad = lax.psum(jnp.sum(grad_normed * unit_rows, axis=0) * scale, "dp")
    term = lax.dot_general(
        columns, normed, (((0,), (0,)), ((), ())), preferred_element_type=jnp.float32
    )
    kv_grad = lax.psum_scatter(
        (term * scale).astype(jnp.bfloat16), "dp", scatter_dimension=0, tiled=True
    )
    rows_each = tokens // sections
    own_top = lax.dynamic_slice_in_dim(
        top_grad[0], lax.axis_index("pipe") * rows_each, rows_each, 0
    )
    total = own_top.astype(jnp.float32)
    suffixes = [None] * sections
    for section in reversed(range(sections)):
        total = total + parts[section].astype(jnp.float32)
        suffixes[section] = total.astype(jnp.bfloat16)
    section_grads = lax.all_to_all(jnp.stack(suffixes), "pipe", 0, 0).reshape(tokens, width)
    return (section_grads[None, None], kv_grad[None], gain_grad[None])


def solution(mesh):
    placed = (
        P("pipe", "dp", None, "tensor"),
        P("pipe", "tensor"),
        P("pipe", "dp", None, "tensor"),
        P("pipe", "dp", None, "tensor"),
        P("pipe", "dp", None, "tensor"),
        P("pipe", "dp", None, "tensor"),
        P("pipe", "dp", "tensor"),
        P("dp", None, "tensor"),
        P("dp", None),
    )
    return jax.shard_map(
        body,
        mesh=mesh,
        in_specs=placed,
        out_specs=(P("pipe", "dp", None, "tensor"), P("pipe", "dp", "tensor"), P("pipe", "tensor")),
        check_vma=False,
    )
```

```python
import functools

import jax
import jax.numpy as jnp
from jax import lax
from jax.experimental import pallas as pl
from jax.experimental.pallas import tpu as pltpu
from jax.sharding import PartitionSpec as P

D = 8192
H = 64
KVH = 8
HD = 128
GROUP = H // KVH
EPSILON = 1e-05
EXTRA = 16
LOG2E = 1.4426950408889634
F32 = jnp.float32
BF16 = jnp.bfloat16
VMEM = pl.BlockSpec(memory_space=pltpu.VMEM)
SMEM = pl.BlockSpec(memory_space=pltpu.SMEM)
ANY = pl.BlockSpec(memory_space=pl.ANY)
MIB = 1024 * 1024
PARAMS = pltpu.CompilerParams(vmem_limit_bytes=20 * MIB)
WHOLE = pltpu.CompilerParams(vmem_limit_bytes=60 * MIB)


def nt(a, b):
    return lax.dot_general(a, b, (((1,), (1,)), ((), ())), preferred_element_type=F32)


def tn(a, b):
    return lax.dot_general(a, b, (((0,), (0,)), ((), ())), preferred_element_type=F32)


def nn(a, b):
    return jnp.dot(a, b, preferred_element_type=F32)


def to_row(column):
    size = column.shape[0]
    across = lax.broadcasted_iota(jnp.int32, (size, size), 0)
    down = lax.broadcasted_iota(jnp.int32, (size, size), 1)
    return jnp.sum(jnp.where(across == down, column, 0.0), axis=0, keepdims=True)


def to_column(row):
    size = row.shape[1]
    across = lax.broadcasted_iota(jnp.int32, (size, size), 0)
    down = lax.broadcasted_iota(jnp.int32, (size, size), 1)
    return jnp.sum(jnp.where(across == down, row, 0.0), axis=1, keepdims=True)


def in_three_rows(row):
    high = row.astype(BF16).astype(F32)
    middle = (row - high).astype(BF16).astype(F32)
    low = row - high - middle
    place = lax.broadcasted_iota(jnp.int32, (EXTRA, row.shape[1]), 0)
    rows = jnp.where(place == 0, high, jnp.where(place == 1, middle, jnp.where(place == 2, low, 0.0)))
    return rows.astype(BF16)


def attention_kernel(lengths, query, key, value, out_grad, inputs, out, *scratch):
    query_v, key_v, value_v, grad_v, inputs_v, result, sems, out_sems = scratch
    tokens = query.shape[0]
    loads = [pltpu.make_async_copy(key, key_v, sems.at[0]), pltpu.make_async_copy(value, value_v, sems.at[1])]
    step = 2 * HD
    for part in range(GROUP // 2):
        span = pl.ds(part * step, step)
        loads.append(pltpu.make_async_copy(query.at[:, span], query_v.at[:, span], sems.at[2 + 2 * part]))
        loads.append(pltpu.make_async_copy(out_grad.at[:, span], grad_v.at[:, span], sems.at[3 + 2 * part]))
    loads.append(pltpu.make_async_copy(inputs, inputs_v, sems.at[2 + GROUP]))
    for load in loads:
        load.start()
    key_place = lax.broadcasted_iota(jnp.int32, (tokens, tokens), 0)
    query_place = lax.broadcasted_iota(jnp.int32, (tokens, tokens), 1)
    allowed = key_place <= query_place
    bound = 0
    for index in range(lengths.shape[1]):
        bound = bound + lengths[0, index]
        allowed &= (key_place >= bound) == (query_place >= bound)
    bias = jnp.where(allowed, 0.0, -1e30)
    factor = HD ** (-0.5)
    loads[0].wait()
    loads[1].wait()
    keys, values = key_v[...], value_v[...]
    grad_keys = jnp.zeros((tokens, HD), F32)
    grad_values = jnp.zeros((tokens, HD), F32)
    for head in range(GROUP):
        if head % 2 == 0:
            loads[2 + head].wait()
            loads[3 + head].wait()
        columns = slice(head * HD, (head + 1) * HD)
        rows, grads = query_v[:, columns], grad_v[:, columns]
        scores = nt(keys, rows) + bias
        top = jnp.max(scores, axis=0, keepdims=True)
        expos = jnp.exp2((scores - top) * (factor * LOG2E))
        probs = expos * (1.0 / jnp.sum(expos, axis=0, keepdims=True))
        grad_values += nn(probs.astype(BF16), grads)
        grad_probs = nt(values, grads)
        centre = jnp.sum(probs * grad_probs, axis=0, keepdims=True)
        grad_scores = (probs * ((grad_probs - centre) * factor)).astype(BF16)
        grad_keys += nn(grad_scores, rows)
    loads[2 + GROUP].wait()
    wide = inputs_v[...].astype(F32)
    extra = in_three_rows(to_row(jnp.sum(wide * wide, axis=1, keepdims=True)))
    grad_keys, grad_values = grad_keys.astype(BF16), grad_values.astype(BF16)
    result[:tokens, :HD] = grad_keys
    result[:tokens, HD:] = grad_values
    result[tokens:, :] = extra
    stores = [
        pltpu.make_async_copy(result, out.at[copy], out_sems.at[copy])
        for copy in range(out.shape[0])
    ]
    for store in stores:
        store.start()
    for store in stores:
        store.wait()


def project_kernel(order, grad_kv, *refs):
    pieces, (rows, gain), outs = refs[:4], refs[4:6], refs[6:11]
    mine, for_near, for_far, scaled_out, prods = outs
    inverse_out = refs[11]
    tokens, width = rows.shape
    half = width // 2
    sums = jnp.zeros((EXTRA, tokens), F32)
    for block in range(grad_kv.shape[0]):
        sums = sums + grad_kv[block, tokens:, :].astype(F32)
    inverse = to_column(1.0 / jnp.sqrt(jnp.sum(sums, axis=0, keepdims=True) * (1.0 / D) + EPSILON))
    inverse_out[...] = inverse
    places = ((mine, 0), (for_near, 0), (for_far, 0), (for_far, 1))
    for place, (target, slot) in enumerate(places):
        for part in range(2):
            span = slice(part * 2 * HD, (part + 1) * 2 * HD)
            target[slot, :tokens, span] = grad_kv[order[2 * place + part], :tokens, :]
        target[slot, tokens:, :] = jnp.zeros((EXTRA, half), BF16)
    total = None
    for (target, slot), piece in zip(places, pieces):
        term = nn(target[slot, :tokens, :], piece[...])
        total = term if total is None else total + term
    unit = rows[...].astype(F32) * inverse
    scaled = total * gain[...]
    scaled_out[...] = scaled
    normed = (unit * gain[...]).astype(BF16)
    gains = in_three_rows(jnp.sum(total * unit, axis=0, keepdims=True))
    for target, slot in ((mine, 1), (for_near, 1), (for_far, 2)):
        for part in range(2):
            span = slice(part * half, (part + 1) * half)
            target[slot + part, :tokens, :] = normed[:, span]
            target[slot + part, tokens:, :] = gains[:, span]
    sums = to_row(jnp.sum(scaled * unit, axis=1, keepdims=True))
    for copy in range(prods.shape[0]):
        prods[copy] = sums


def contrib_kernel(prods, scaled, rows, inverse, out):
    mean = to_column(jnp.sum(prods[...], axis=0) * (1.0 / D))
    scale = inverse[...]
    unit = rows[...].astype(F32) * scale
    out[...] = ((scaled[...] - unit * mean) * scale).astype(BF16)


def term_kernel(scale, mine, near, far, diagonal, out, gain_out):
    tokens = mine.shape[1] - EXTRA
    half = mine.shape[2]
    sources = ((mine, 0, 1), (near, 0, 1), (far, 0, 2), (diagonal, 0, 1))
    for part in range(2):
        span = slice(part * half, (part + 1) * half)
        total = None
        sums = []
        for source, share, normed in sources:
            term = tn(source[share, :tokens, :], source[normed + part, :tokens, :])
            term = (term * scale).astype(BF16).astype(F32)
            total = term if total is None else total + term
            extra = source[normed + part, tokens:, :].astype(F32)
            sums.append(jnp.sum(extra, axis=0, keepdims=True))
        out[:, span] = total.astype(BF16)
        gain_out[:, span] = ((sums[0] + sums[1]) + (sums[2] + sums[3])) * scale


def suffix_kernel(parts, above, out):
    total = above[...].astype(F32)
    for part in reversed(range(parts.shape[0])):
        total = total + parts[part].astype(F32)
        out[part] = total.astype(BF16)


def swap(value, axis, distance):
    count = lax.axis_size(axis)
    return lax.ppermute(value, axis, [(source, source ^ distance) for source in range(count)])


def body(
    inputs,
    norm_gain,
    queries,
    saved_keys,
    saved_values,
    attn_out_grad,
    kv_projection,
    top_grad,
    doc_lengths,
):
    tensor, sections, dp = lax.axis_size("tensor"), lax.axis_size("pipe"), lax.axis_size("dp")
    rows = inputs[0, 0]
    tokens, width = rows.shape
    mine, stage = lax.axis_index("dp"), lax.axis_index("pipe")

    own = kv_projection[0]
    far = swap(own, "dp", 2)
    near = swap(own, "dp", 1)

    copies = pl.pallas_call(
        attention_kernel,
        out_shape=jax.ShapeDtypeStruct((tensor, tokens + EXTRA, 2 * HD), BF16),
        in_specs=[SMEM] + [ANY] * 5,
        out_specs=ANY,
        scratch_shapes=[
            pltpu.VMEM((tokens, GROUP * HD), BF16),
            pltpu.VMEM((tokens, HD), BF16),
            pltpu.VMEM((tokens, HD), BF16),
            pltpu.VMEM((tokens, GROUP * HD), BF16),
            pltpu.VMEM((tokens, width), BF16),
            pltpu.VMEM((tokens + EXTRA, 2 * HD), BF16),
            pltpu.SemaphoreType.DMA((3 + GROUP,)),
            pltpu.SemaphoreType.DMA((tensor,)),
        ],
        compiler_params=WHOLE,
    )(doc_lengths, queries[0, 0], saved_keys[0, 0], saved_values[0, 0], attn_out_grad[0, 0], rows)
    grad_kv = lax.all_to_all(copies, "tensor", 0, 0)
    far, grad_kv = lax.optimization_barrier((far, grad_kv))
    far_near = swap(far, "dp", 1)
    order = [2 * (mine ^ place) + part for place in range(dp) for part in range(2)]

    mixed = tokens + EXTRA
    own_set, for_near, for_far, scaled, prods, inverse = pl.pallas_call(
        project_kernel,
        out_shape=(
            jax.ShapeDtypeStruct((3, mixed, width // 2), BF16),
            jax.ShapeDtypeStruct((3, mixed, width // 2), BF16),
            jax.ShapeDtypeStruct((4, mixed, width // 2), BF16),
            jax.ShapeDtypeStruct((tokens, width), F32),
            jax.ShapeDtypeStruct((tensor, 1, tokens), F32),
            jax.ShapeDtypeStruct((tokens, 1), F32),
        ),
        in_specs=[SMEM] + [VMEM] * 7,
        out_specs=(VMEM,) * 6,
        compiler_params=PARAMS,
    )(jnp.stack(order).astype(jnp.int32), grad_kv, own, near, far, far_near, rows, norm_gain)
    prods = lax.all_to_all(prods, "tensor", 0, 0)

    near_set = swap(for_near, "dp", 1)
    far_set = swap(for_far, "dp", 2)

    def local(kernel, shape, *operands):
        return pl.pallas_call(
            kernel,
            out_shape=jax.ShapeDtypeStruct(shape, BF16),
            in_specs=[VMEM] * len(operands),
            out_specs=VMEM,
            compiler_params=PARAMS,
        )(*operands)

    prods, near_set = lax.optimization_barrier((prods, near_set))
    contrib = local(contrib_kernel, (tokens, width), prods, scaled, rows, inverse)
    small = tokens // sections
    own_top = lax.dynamic_slice_in_dim(top_grad[0], stage * small, small, 0)
    parts = lax.all_to_all(contrib.reshape(sections, small, width), "pipe", 0, 0)
    parts, far_set = lax.optimization_barrier((parts, far_set))
    diagonal_set = swap(far_set[1:], "dp", 1)
    suffixes = local(suffix_kernel, parts.shape, parts, own_top)
    section_grads = lax.all_to_all(suffixes, "pipe", 0, 0).reshape(tokens, width)
    kv_grad, gain_grad = pl.pallas_call(
        functools.partial(term_kernel, (dp * tokens) ** (-0.5)),
        out_shape=(
            jax.ShapeDtypeStruct((tensor // dp * 2 * HD, width), BF16),
            jax.ShapeDtypeStruct((1, width), F32),
        ),
        in_specs=[VMEM] * 4,
        out_specs=(VMEM, VMEM),
        compiler_params=PARAMS,
    )(own_set, near_set, far_set, diagonal_set)

    return (section_grads[None, None], kv_grad[None], gain_grad)


def solution(mesh):
    placed = (
        P("pipe", "dp", None, "tensor"),
        P("pipe", "tensor"),
        P("pipe", "dp", None, "tensor"),
        P("pipe", "dp", None, "tensor"),
        P("pipe", "dp", None, "tensor"),
        P("pipe", "dp", None, "tensor"),
        P("pipe", "dp", "tensor"),
        P("dp", None, "tensor"),
        P("dp", None),
    )
    return jax.shard_map(
        body,
        mesh=mesh,
        in_specs=placed,
        out_specs=(P("pipe", "dp", None, "tensor"), P("pipe", "dp", "tensor"), P("pipe", "tensor")),
        check_vma=False,
    )
```

```python
import functools

import jax
import jax.numpy as jnp
from jax import lax
from jax.experimental import pallas as pl
from jax.experimental.pallas import tpu as pltpu
from jax.sharding import PartitionSpec as P

D = 8192
H = 64
KVH = 8
HD = 128
GROUP = H // KVH
EPSILON = 1e-05
EXTRA = 16
LOG2E = 1.4426950408889634
F32 = jnp.float32
BF16 = jnp.bfloat16
VMEM = pl.BlockSpec(memory_space=pltpu.VMEM)
SMEM = pl.BlockSpec(memory_space=pltpu.SMEM)
ANY = pl.BlockSpec(memory_space=pl.ANY)
MIB = 1024 * 1024
PARAMS = pltpu.CompilerParams(vmem_limit_bytes=20 * MIB)
SMALL = pltpu.CompilerParams(vmem_limit_bytes=12 * MIB)
WHOLE = pltpu.CompilerParams(vmem_limit_bytes=60 * MIB)


def nt(a, b):
    return lax.dot_general(a, b, (((1,), (1,)), ((), ())), preferred_element_type=F32)


def tn(a, b):
    return lax.dot_general(a, b, (((0,), (0,)), ((), ())), preferred_element_type=F32)


def nn(a, b):
    return jnp.dot(a, b, preferred_element_type=F32)


def to_row(column):
    size = column.shape[0]
    across = lax.broadcasted_iota(jnp.int32, (size, size), 0)
    down = lax.broadcasted_iota(jnp.int32, (size, size), 1)
    return jnp.sum(jnp.where(across == down, column, 0.0), axis=0, keepdims=True)


def to_column(row):
    size = row.shape[1]
    across = lax.broadcasted_iota(jnp.int32, (size, size), 0)
    down = lax.broadcasted_iota(jnp.int32, (size, size), 1)
    return jnp.sum(jnp.where(across == down, row, 0.0), axis=1, keepdims=True)


def in_three_rows(row):
    high = row.astype(BF16).astype(F32)
    middle = (row - high).astype(BF16).astype(F32)
    low = row - high - middle
    place = lax.broadcasted_iota(jnp.int32, (EXTRA, row.shape[1]), 0)
    rows = jnp.where(place == 0, high, jnp.where(place == 1, middle, jnp.where(place == 2, low, 0.0)))
    return rows.astype(BF16)


def attention_kernel(lengths, query, key, value, out_grad, inputs, out, *scratch):
    query_v, key_v, value_v, grad_v, inputs_v, result, sems, out_sems = scratch
    tokens = query.shape[0]
    loads = [pltpu.make_async_copy(key, key_v, sems.at[0]), pltpu.make_async_copy(value, value_v, sems.at[1])]
    step = 2 * HD
    for part in range(GROUP // 2):
        span = pl.ds(part * step, step)
        loads.append(pltpu.make_async_copy(query.at[:, span], query_v.at[:, span], sems.at[2 + 2 * part]))
        loads.append(pltpu.make_async_copy(out_grad.at[:, span], grad_v.at[:, span], sems.at[3 + 2 * part]))
    loads.append(pltpu.make_async_copy(inputs, inputs_v, sems.at[2 + GROUP]))
    for load in loads:
        load.start()
    key_place = lax.broadcasted_iota(jnp.int32, (tokens, tokens), 0)
    query_place = lax.broadcasted_iota(jnp.int32, (tokens, tokens), 1)
    allowed = key_place <= query_place
    bound = 0
    for index in range(lengths.shape[1]):
        bound = bound + lengths[0, index]
        allowed &= (key_place >= bound) == (query_place >= bound)
    bias = jnp.where(allowed, 0.0, -1e30)
    factor = HD ** (-0.5)
    loads[0].wait()
    loads[1].wait()
    keys, values = key_v[...], value_v[...]
    grad_keys = jnp.zeros((tokens, HD), F32)
    grad_values = jnp.zeros((tokens, HD), F32)
    for head in range(GROUP):
        if head % 2 == 0:
            loads[2 + head].wait()
            loads[3 + head].wait()
        columns = slice(head * HD, (head + 1) * HD)
        rows, grads = query_v[:, columns], grad_v[:, columns]
        scores = nt(keys, rows) + bias
        top = jnp.max(scores, axis=0, keepdims=True)
        expos = jnp.exp2((scores - top) * (factor * LOG2E))
        probs = expos * (1.0 / jnp.sum(expos, axis=0, keepdims=True))
        grad_values += nn(probs.astype(BF16), grads)
        grad_probs = nt(values, grads)
        centre = jnp.sum(probs * grad_probs, axis=0, keepdims=True)
        grad_scores = (probs * ((grad_probs - centre) * factor)).astype(BF16)
        grad_keys += nn(grad_scores, rows)
    loads[2 + GROUP].wait()
    wide = inputs_v[...].astype(F32)
    extra = in_three_rows(to_row(jnp.sum(wide * wide, axis=1, keepdims=True)))
    grad_keys, grad_values = grad_keys.astype(BF16), grad_values.astype(BF16)
    result[:tokens, :HD] = grad_keys
    result[:tokens, HD:] = grad_values
    result[tokens:, :] = extra
    stores = [
        pltpu.make_async_copy(result, out.at[copy], out_sems.at[copy])
        for copy in range(out.shape[0])
    ]
    for store in stores:
        store.start()
    for store in stores:
        store.wait()


def gather_kernel(order, grad_kv, own, near, far, rows, gain, *outs):
    mine, for_near, for_far, for_diagonal, total_out, inverse_out = outs
    tokens, width = rows.shape
    half = width // 2
    sums = jnp.zeros((EXTRA, tokens), F32)
    for block in range(grad_kv.shape[0]):
        sums = sums + grad_kv[block, tokens:, :].astype(F32)
    inverse = to_column(1.0 / jnp.sqrt(jnp.sum(sums, axis=0, keepdims=True) * (1.0 / D) + EPSILON))
    inverse_out[...] = inverse
    for place, target in enumerate((mine, for_near, for_far, for_diagonal)):
        for part in range(2):
            span = slice(part * 2 * HD, (part + 1) * 2 * HD)
            target[0, :, span] = grad_kv[order[2 * place + part], :tokens, :]
    total_out[...] = (
        nn(mine[0], own[...]) + nn(for_near[0], near[...]) + nn(for_far[0], far[...])
    )
    normed = (rows[...].astype(F32) * inverse * gain[...]).astype(BF16)
    for target in (mine, for_near, for_far):
        target[1] = normed[:, :half]
        target[2] = normed[:, half:]


def project_kernel(part, share, piece, rows, gain, inverse, scaled_out, prods, gains_out):
    total = part[...] + nn(share[0], piece[...])
    unit = rows[...].astype(F32) * inverse[...]
    scaled = total * gain[...]
    scaled_out[...] = scaled
    gains_out[...] = jnp.sum(total * unit, axis=0, keepdims=True)
    sums = to_row(jnp.sum(scaled * unit, axis=1, keepdims=True))
    for copy in range(prods.shape[0]):
        prods[copy] = sums


def contrib_kernel(prods, scaled, rows, inverse, out):
    mean = to_column(jnp.sum(prods[...], axis=0) * (1.0 / D))
    scale = inverse[...]
    unit = rows[...].astype(F32) * scale
    out[...] = ((scaled[...] - unit * mean) * scale).astype(BF16)


def term_kernel(scale, mine, near, far, share, diagonal, out):
    half = mine.shape[2]
    sources = ((mine, mine, 1), (near, near, 1), (far, far, 1), (share, diagonal, 0))
    for part in range(2):
        total = None
        for heads, source, normed in sources:
            term = tn(heads[0], source[normed + part])
            term = (term * scale).astype(BF16).astype(F32)
            total = term if total is None else total + term
        out[:, part * half : (part + 1) * half] = total.astype(BF16)


def suffix_kernel(parts, above, out):
    total = above[...].astype(F32)
    for part in reversed(range(parts.shape[0])):
        total = total + parts[part].astype(F32)
        out[part] = total.astype(BF16)


def copy_kernel(source, out):
    out[...] = source[...]


def swap(value, axis, distance):
    count = lax.axis_size(axis)
    return lax.ppermute(value, axis, [(source, source ^ distance) for source in range(count)])


def body(
    inputs,
    norm_gain,
    queries,
    saved_keys,
    saved_values,
    attn_out_grad,
    kv_projection,
    top_grad,
    doc_lengths,
):
    tensor, sections, dp = lax.axis_size("tensor"), lax.axis_size("pipe"), lax.axis_size("dp")
    rows = inputs[0, 0]
    tokens, width = rows.shape
    mine, stage = lax.axis_index("dp"), lax.axis_index("pipe")

    own = kv_projection[0]
    far = swap(own, "dp", 2)
    near = swap(own, "dp", 1)

    copies = pl.pallas_call(
        attention_kernel,
        out_shape=jax.ShapeDtypeStruct((tensor, tokens + EXTRA, 2 * HD), BF16),
        in_specs=[SMEM] + [ANY] * 5,
        out_specs=ANY,
        scratch_shapes=[
            pltpu.VMEM((tokens, GROUP * HD), BF16),
            pltpu.VMEM((tokens, HD), BF16),
            pltpu.VMEM((tokens, HD), BF16),
            pltpu.VMEM((tokens, GROUP * HD), BF16),
            pltpu.VMEM((tokens, width), BF16),
            pltpu.VMEM((tokens + EXTRA, 2 * HD), BF16),
            pltpu.SemaphoreType.DMA((3 + GROUP,)),
            pltpu.SemaphoreType.DMA((tensor,)),
        ],
        compiler_params=WHOLE,
    )(doc_lengths, queries[0, 0], saved_keys[0, 0], saved_values[0, 0], attn_out_grad[0, 0], rows)
    grad_kv = lax.all_to_all(copies, "tensor", 0, 0)
    far, grad_kv = lax.optimization_barrier((far, grad_kv))
    far_near = swap(far, "dp", 1)
    order = [2 * (mine ^ place) + part for place in range(dp) for part in range(2)]

    def blocks(count):
        return jax.ShapeDtypeStruct((count, tokens, width // 2), BF16)

    wide = jax.ShapeDtypeStruct((tokens, width), F32)
    own_set, for_near, for_far, for_diagonal, total, inverse = pl.pallas_call(
        gather_kernel,
        out_shape=(
            blocks(3),
            blocks(3),
            blocks(3),
            blocks(1),
            wide,
            jax.ShapeDtypeStruct((tokens, 1), F32),
        ),
        in_specs=[SMEM] + [VMEM] * 6,
        out_specs=(VMEM,) * 6,
        compiler_params=PARAMS,
    )(jnp.stack(order).astype(jnp.int32), grad_kv, own, near, far, rows, norm_gain)
    scaled, prods, gains = pl.pallas_call(
        project_kernel,
        out_shape=(
            wide,
            jax.ShapeDtypeStruct((tensor, 1, tokens), F32),
            jax.ShapeDtypeStruct((1, width), F32),
        ),
        in_specs=[VMEM] * 6,
        out_specs=(VMEM,) * 3,
        compiler_params=PARAMS,
    )(total, for_diagonal, far_near, rows, norm_gain, inverse)
    prods = lax.all_to_all(prods, "tensor", 0, 0)

    far_set = swap(for_far, "dp", 2)

    def local(kernel, shape, *operands):
        return pl.pallas_call(
            kernel,
            out_shape=jax.ShapeDtypeStruct(shape, BF16),
            in_specs=[VMEM] * len(operands),
            out_specs=VMEM,
            compiler_params=SMALL,
        )(*operands)

    contrib = local(contrib_kernel, (tokens, width), prods, scaled, rows, inverse)
    small = tokens // sections
    own_top = lax.dynamic_slice_in_dim(top_grad[0], stage * small, small, 0)
    parts = lax.all_to_all(contrib.reshape(sections, small, width), "pipe", 0, 0)
    parts, far_set, gains = lax.optimization_barrier((parts, far_set, gains))
    near_set = swap(for_near, "dp", 1)
    diagonal_share = swap(for_diagonal, "dp", 3)
    diagonal_set = swap(far_set[1:], "dp", 1)
    suffixes = local(suffix_kernel, parts.shape, parts, own_top)
    section_grads = lax.all_to_all(suffixes, "pipe", 0, 0).reshape(tokens, width)
    section_grads = local(copy_kernel, (tokens, width), section_grads)
    scale = (dp * tokens) ** (-0.5)
    kv_grad = pl.pallas_call(
        functools.partial(term_kernel, scale),
        out_shape=jax.ShapeDtypeStruct((tensor // dp * 2 * HD, width), BF16),
        in_specs=[VMEM] * 5,
        out_specs=VMEM,
        compiler_params=SMALL,
    )(own_set, near_set, far_set, diagonal_share, diagonal_set)
    gain_grad = lax.psum(gains * scale, "dp")

    return (section_grads[None, None], kv_grad[None], gain_grad)


def solution(mesh):
    placed = (
        P("pipe", "dp", None, "tensor"),
        P("pipe", "tensor"),
        P("pipe", "dp", None, "tensor"),
        P("pipe", "dp", None, "tensor"),
        P("pipe", "dp", None, "tensor"),
        P("pipe", "dp", None, "tensor"),
        P("pipe", "dp", "tensor"),
        P("dp", None, "tensor"),
        P("dp", None),
    )
    return jax.shard_map(
        body,
        mesh=mesh,
        in_specs=placed,
        out_specs=(P("pipe", "dp", None, "tensor"), P("pipe", "dp", "tensor"), P("pipe", "tensor")),
        check_vma=False,
    )
```

```python
import functools

import jax
import jax.numpy as jnp
from jax import lax
from jax.experimental import pallas as pl
from jax.experimental.pallas import tpu as pltpu
from jax.sharding import PartitionSpec as P

D = 8192
H = 64
KVH = 8
HD = 128
GROUP = H // KVH
EPSILON = 1e-05
EXTRA = 16
LOG2E = 1.4426950408889634
F32 = jnp.float32
BF16 = jnp.bfloat16
VMEM = pl.BlockSpec(memory_space=pltpu.VMEM)
SMEM = pl.BlockSpec(memory_space=pltpu.SMEM)
ANY = pl.BlockSpec(memory_space=pl.ANY)
MIB = 1024 * 1024
PARAMS = pltpu.CompilerParams(vmem_limit_bytes=20 * MIB)
SMALL = pltpu.CompilerParams(vmem_limit_bytes=12 * MIB)
WHOLE = pltpu.CompilerParams(vmem_limit_bytes=60 * MIB)


def nt(a, b):
    return lax.dot_general(a, b, (((1,), (1,)), ((), ())), preferred_element_type=F32)


def tn(a, b):
    return lax.dot_general(a, b, (((0,), (0,)), ((), ())), preferred_element_type=F32)


def nn(a, b):
    return jnp.dot(a, b, preferred_element_type=F32)


def to_row(column):
    size = column.shape[0]
    across = lax.broadcasted_iota(jnp.int32, (size, size), 0)
    down = lax.broadcasted_iota(jnp.int32, (size, size), 1)
    return jnp.sum(jnp.where(across == down, column, 0.0), axis=0, keepdims=True)


def to_column(row):
    size = row.shape[1]
    across = lax.broadcasted_iota(jnp.int32, (size, size), 0)
    down = lax.broadcasted_iota(jnp.int32, (size, size), 1)
    return jnp.sum(jnp.where(across == down, row, 0.0), axis=1, keepdims=True)


def in_three_rows(row):
    high = row.astype(BF16).astype(F32)
    middle = (row - high).astype(BF16).astype(F32)
    low = row - high - middle
    place = lax.broadcasted_iota(jnp.int32, (EXTRA, row.shape[1]), 0)
    rows = jnp.where(place == 0, high, jnp.where(place == 1, middle, jnp.where(place == 2, low, 0.0)))
    return rows.astype(BF16)


def attention_kernel(lengths, query, key, value, out_grad, inputs, out, *scratch):
    query_v, key_v, value_v, grad_v, inputs_v, result, sems, out_sems = scratch
    tokens = query.shape[0]
    loads = [pltpu.make_async_copy(key, key_v, sems.at[0]), pltpu.make_async_copy(value, value_v, sems.at[1])]
    step = 2 * HD
    for part in range(GROUP // 2):
        span = pl.ds(part * step, step)
        loads.append(pltpu.make_async_copy(query.at[:, span], query_v.at[:, span], sems.at[2 + 2 * part]))
        loads.append(pltpu.make_async_copy(out_grad.at[:, span], grad_v.at[:, span], sems.at[3 + 2 * part]))
    loads.append(pltpu.make_async_copy(inputs, inputs_v, sems.at[2 + GROUP]))
    for load in loads:
        load.start()
    key_place = lax.broadcasted_iota(jnp.int32, (tokens, tokens), 0)
    query_place = lax.broadcasted_iota(jnp.int32, (tokens, tokens), 1)
    allowed = key_place <= query_place
    bound = 0
    for index in range(lengths.shape[1]):
        bound = bound + lengths[0, index]
        allowed &= (key_place >= bound) == (query_place >= bound)
    bias = jnp.where(allowed, 0.0, -1e30)
    factor = HD ** (-0.5)
    loads[0].wait()
    loads[1].wait()
    keys, values = key_v[...], value_v[...]
    grad_keys = jnp.zeros((tokens, HD), F32)
    grad_values = jnp.zeros((tokens, HD), F32)
    for head in range(GROUP):
        if head % 2 == 0:
            loads[2 + head].wait()
            loads[3 + head].wait()
        columns = slice(head * HD, (head + 1) * HD)
        rows, grads = query_v[:, columns], grad_v[:, columns]
        scores = nt(keys, rows) + bias
        top = jnp.max(scores, axis=0, keepdims=True)
        expos = jnp.exp2((scores - top) * (factor * LOG2E))
        probs = expos * (1.0 / jnp.sum(expos, axis=0, keepdims=True))
        grad_values += nn(probs.astype(BF16), grads)
        grad_probs = nt(values, grads)
        centre = jnp.sum(probs * grad_probs, axis=0, keepdims=True)
        grad_scores = (probs * ((grad_probs - centre) * factor)).astype(BF16)
        grad_keys += nn(grad_scores, rows)
    loads[2 + GROUP].wait()
    wide = inputs_v[...].astype(F32)
    extra = in_three_rows(to_row(jnp.sum(wide * wide, axis=1, keepdims=True)))
    grad_keys, grad_values = grad_keys.astype(BF16), grad_values.astype(BF16)
    result[:tokens, :HD] = grad_keys
    result[:tokens, HD:] = grad_values
    result[tokens:, :] = extra
    stores = [
        pltpu.make_async_copy(result, out.at[copy], out_sems.at[copy])
        for copy in range(out.shape[0])
    ]
    for store in stores:
        store.start()
    for store in stores:
        store.wait()


def gather_kernel(order, grad_kv, own, near, far, rows, gain, *outs):
    mine, for_near, for_far, for_diagonal, total_out, inverse_out = outs
    tokens, width = rows.shape
    half = width // 2
    sums = jnp.zeros((EXTRA, tokens), F32)
    for block in range(grad_kv.shape[0]):
        sums = sums + grad_kv[block, tokens:, :].astype(F32)
    inverse = to_column(1.0 / jnp.sqrt(jnp.sum(sums, axis=0, keepdims=True) * (1.0 / D) + EPSILON))
    inverse_out[...] = inverse
    for place, target in enumerate((mine, for_near, for_far, for_diagonal)):
        for part in range(2):
            span = slice(part * 2 * HD, (part + 1) * 2 * HD)
            target[0, :, span] = grad_kv[order[2 * place + part], :tokens, :]
    total_out[...] = (
        nn(mine[0], own[...]) + nn(for_near[0], near[...]) + nn(for_far[0], far[...])
    )
    normed = (rows[...].astype(F32) * inverse * gain[...]).astype(BF16)
    for target in (mine, for_near, for_far):
        target[1] = normed[:, :half]
        target[2] = normed[:, half:]


def project_kernel(part, share, piece, rows, gain, inverse, scaled_out, prods, gains_out):
    total = part[...] + nn(share[0], piece[...])
    unit = rows[...].astype(F32) * inverse[...]
    scaled = total * gain[...]
    scaled_out[...] = scaled
    gains_out[...] = jnp.sum(total * unit, axis=0, keepdims=True)
    sums = to_row(jnp.sum(scaled * unit, axis=1, keepdims=True))
    for copy in range(prods.shape[0]):
        prods[copy] = sums


def contrib_kernel(prods, scaled, rows, inverse, out):
    mean = to_column(jnp.sum(prods[...], axis=0) * (1.0 / D))
    scale = inverse[...]
    unit = rows[...].astype(F32) * scale
    out[...] = ((scaled[...] - unit * mean) * scale).astype(BF16)


def term_kernel(scale, mine, near, far, share, diagonal, out):
    half = mine.shape[2]
    sources = ((mine, mine, 1), (near, near, 1), (far, far, 1), (share, diagonal, 0))
    for part in range(2):
        total = None
        for heads, source, normed in sources:
            term = tn(heads[0], source[normed + part])
            term = (term * scale).astype(BF16).astype(F32)
            total = term if total is None else total + term
        out[:, part * half : (part + 1) * half] = total.astype(BF16)


def suffix_kernel(parts, above, out):
    total = above[...].astype(F32)
    for part in reversed(range(parts.shape[0])):
        total = total + parts[part].astype(F32)
        out[part] = total.astype(BF16)


def copy_kernel(source, out):
    out[...] = source[...]


def swap(value, axis, distance):
    count = lax.axis_size(axis)
    return lax.ppermute(value, axis, [(source, source ^ distance) for source in range(count)])


def body(
    inputs,
    norm_gain,
    queries,
    saved_keys,
    saved_values,
    attn_out_grad,
    kv_projection,
    top_grad,
    doc_lengths,
):
    tensor, sections, dp = lax.axis_size("tensor"), lax.axis_size("pipe"), lax.axis_size("dp")
    rows = inputs[0, 0]
    tokens, width = rows.shape
    mine, stage = lax.axis_index("dp"), lax.axis_index("pipe")

    own = kv_projection[0]
    far = swap(own, "dp", 2)

    copies = pl.pallas_call(
        attention_kernel,
        out_shape=jax.ShapeDtypeStruct((tensor, tokens + EXTRA, 2 * HD), BF16),
        in_specs=[SMEM] + [ANY] * 5,
        out_specs=ANY,
        scratch_shapes=[
            pltpu.VMEM((tokens, GROUP * HD), BF16),
            pltpu.VMEM((tokens, HD), BF16),
            pltpu.VMEM((tokens, HD), BF16),
            pltpu.VMEM((tokens, GROUP * HD), BF16),
            pltpu.VMEM((tokens, width), BF16),
            pltpu.VMEM((tokens + EXTRA, 2 * HD), BF16),
            pltpu.SemaphoreType.DMA((3 + GROUP,)),
            pltpu.SemaphoreType.DMA((tensor,)),
        ],
        compiler_params=WHOLE,
        cost_estimate=pl.CostEstimate(flops=int(3e+10), bytes_accessed=4000000, transcendentals=0),
    )(doc_lengths, queries[0, 0], saved_keys[0, 0], saved_values[0, 0], attn_out_grad[0, 0], rows)
    copies, whole = lax.optimization_barrier((copies, own))
    grad_kv = lax.all_to_all(copies, "tensor", 0, 0)
    near = swap(whole, "dp", 1)
    far_near = swap(far, "dp", 1)
    order = [2 * (mine ^ place) + part for place in range(dp) for part in range(2)]

    def blocks(count):
        return jax.ShapeDtypeStruct((count, tokens, width // 2), BF16)

    wide = jax.ShapeDtypeStruct((tokens, width), F32)
    own_set, for_near, for_far, for_diagonal, total, inverse = pl.pallas_call(
        gather_kernel,
        out_shape=(
            blocks(3),
            blocks(3),
            blocks(3),
            blocks(1),
            wide,
            jax.ShapeDtypeStruct((tokens, 1), F32),
        ),
        in_specs=[SMEM] + [VMEM] * 6,
        out_specs=(VMEM,) * 6,
        compiler_params=PARAMS,
        cost_estimate=pl.CostEstimate(flops=int(3e+10), bytes_accessed=0, transcendentals=0),
    )(jnp.stack(order).astype(jnp.int32), grad_kv, own, near, far, rows, norm_gain)
    scaled, prods, gains = pl.pallas_call(
        project_kernel,
        out_shape=(
            wide,
            jax.ShapeDtypeStruct((tensor, 1, tokens), F32),
            jax.ShapeDtypeStruct((1, width), F32),
        ),
        in_specs=[VMEM] * 6,
        out_specs=(VMEM,) * 3,
        compiler_params=PARAMS,
    )(total, for_diagonal, far_near, rows, norm_gain, inverse)
    prods = lax.all_to_all(prods, "tensor", 0, 0)

    far_set = swap(for_far, "dp", 2)

    def local(kernel, shape, *operands):
        return pl.pallas_call(
            kernel,
            out_shape=jax.ShapeDtypeStruct(shape, BF16),
            in_specs=[VMEM] * len(operands),
            out_specs=VMEM,
            compiler_params=SMALL,
        )(*operands)

    contrib = local(contrib_kernel, (tokens, width), prods, scaled, rows, inverse)
    small = tokens // sections
    own_top = lax.dynamic_slice_in_dim(top_grad[0], stage * small, small, 0)
    parts = lax.all_to_all(contrib.reshape(sections, small, width), "pipe", 0, 0)
    parts, far_set, gains = lax.optimization_barrier((parts, far_set, gains))
    near_set = swap(for_near, "dp", 1)
    diagonal_share = swap(for_diagonal, "dp", 3)
    diagonal_set = swap(far_set[1:], "dp", 1)
    suffixes = local(suffix_kernel, parts.shape, parts, own_top)
    section_grads = lax.all_to_all(suffixes, "pipe", 0, 0).reshape(tokens, width)
    section_grads = local(copy_kernel, (tokens, width), section_grads)
    scale = (dp * tokens) ** (-0.5)
    kv_grad = pl.pallas_call(
        functools.partial(term_kernel, scale),
        out_shape=jax.ShapeDtypeStruct((tensor // dp * 2 * HD, width), BF16),
        in_specs=[VMEM] * 5,
        out_specs=VMEM,
        compiler_params=SMALL,
    )(own_set, near_set, far_set, diagonal_share, diagonal_set)
    gain_grad = lax.psum(gains * scale, "dp")

    return (section_grads[None, None], kv_grad[None], gain_grad)


def solution(mesh):
    placed = (
        P("pipe", "dp", None, "tensor"),
        P("pipe", "tensor"),
        P("pipe", "dp", None, "tensor"),
        P("pipe", "dp", None, "tensor"),
        P("pipe", "dp", None, "tensor"),
        P("pipe", "dp", None, "tensor"),
        P("pipe", "dp", "tensor"),
        P("dp", None, "tensor"),
        P("dp", None),
    )
    return jax.shard_map(
        body,
        mesh=mesh,
        in_specs=placed,
        out_specs=(P("pipe", "dp", None, "tensor"), P("pipe", "dp", "tensor"), P("pipe", "tensor")),
        check_vma=False,
    )
```

```python
import functools

import jax
import jax.numpy as jnp
from jax import lax
from jax.experimental import pallas as pl
from jax.experimental.pallas import tpu as pltpu
from jax.sharding import PartitionSpec as P

D = 8192
H = 64
KVH = 8
HD = 128
GROUP = H // KVH
EPSILON = 1e-05
EXTRA = 16
LOG2E = 1.4426950408889634
F32 = jnp.float32
BF16 = jnp.bfloat16
VMEM = pl.BlockSpec(memory_space=pltpu.VMEM)
SMEM = pl.BlockSpec(memory_space=pltpu.SMEM)
ANY = pl.BlockSpec(memory_space=pl.ANY)
MIB = 1024 * 1024
PARAMS = pltpu.CompilerParams(vmem_limit_bytes=20 * MIB)
SMALL = pltpu.CompilerParams(vmem_limit_bytes=12 * MIB)
WHOLE = pltpu.CompilerParams(vmem_limit_bytes=60 * MIB)


def nt(a, b):
    return lax.dot_general(a, b, (((1,), (1,)), ((), ())), preferred_element_type=F32)


def tn(a, b):
    return lax.dot_general(a, b, (((0,), (0,)), ((), ())), preferred_element_type=F32)


def nn(a, b):
    return jnp.dot(a, b, preferred_element_type=F32)


def to_row(column):
    size = column.shape[0]
    across = lax.broadcasted_iota(jnp.int32, (size, size), 0)
    down = lax.broadcasted_iota(jnp.int32, (size, size), 1)
    return jnp.sum(jnp.where(across == down, column, 0.0), axis=0, keepdims=True)


def to_column(row):
    size = row.shape[1]
    across = lax.broadcasted_iota(jnp.int32, (size, size), 0)
    down = lax.broadcasted_iota(jnp.int32, (size, size), 1)
    return jnp.sum(jnp.where(across == down, row, 0.0), axis=1, keepdims=True)


def in_three_rows(row):
    high = row.astype(BF16).astype(F32)
    middle = (row - high).astype(BF16).astype(F32)
    low = row - high - middle
    place = lax.broadcasted_iota(jnp.int32, (EXTRA, row.shape[1]), 0)
    rows = jnp.where(place == 0, high, jnp.where(place == 1, middle, jnp.where(place == 2, low, 0.0)))
    return rows.astype(BF16)


def attention_kernel(lengths, query, key, value, out_grad, inputs, out, *scratch):
    query_v, key_v, value_v, grad_v, inputs_v, result, sems, out_sems = scratch
    tokens = query.shape[0]
    loads = [pltpu.make_async_copy(key, key_v, sems.at[0]), pltpu.make_async_copy(value, value_v, sems.at[1])]
    step = 2 * HD
    for part in range(GROUP // 2):
        span = pl.ds(part * step, step)
        loads.append(pltpu.make_async_copy(query.at[:, span], query_v.at[:, span], sems.at[2 + 2 * part]))
        loads.append(pltpu.make_async_copy(out_grad.at[:, span], grad_v.at[:, span], sems.at[3 + 2 * part]))
    loads.append(pltpu.make_async_copy(inputs, inputs_v, sems.at[2 + GROUP]))
    for load in loads:
        load.start()
    key_place = lax.broadcasted_iota(jnp.int32, (tokens, tokens), 0)
    query_place = lax.broadcasted_iota(jnp.int32, (tokens, tokens), 1)
    allowed = key_place <= query_place
    bound = 0
    for index in range(lengths.shape[1]):
        bound = bound + lengths[0, index]
        allowed &= (key_place >= bound) == (query_place >= bound)
    bias = jnp.where(allowed, 0.0, -1e30)
    factor = HD ** (-0.5)
    loads[0].wait()
    loads[1].wait()
    keys, values = key_v[...], value_v[...]
    grad_keys = jnp.zeros((tokens, HD), F32)
    grad_values = jnp.zeros((tokens, HD), F32)
    for head in range(GROUP):
        if head % 2 == 0:
            loads[2 + head].wait()
            loads[3 + head].wait()
        columns = slice(head * HD, (head + 1) * HD)
        rows, grads = query_v[:, columns], grad_v[:, columns]
        scores = nt(keys, rows) + bias
        top = jnp.max(scores, axis=0, keepdims=True)
        expos = jnp.exp2((scores - top) * (factor * LOG2E))
        probs = expos * (1.0 / jnp.sum(expos, axis=0, keepdims=True))
        grad_values += nn(probs.astype(BF16), grads)
        grad_probs = nt(values, grads)
        centre = jnp.sum(probs * grad_probs, axis=0, keepdims=True)
        grad_scores = (probs * ((grad_probs - centre) * factor)).astype(BF16)
        grad_keys += nn(grad_scores, rows)
    loads[2 + GROUP].wait()
    wide = inputs_v[...].astype(F32)
    extra = in_three_rows(to_row(jnp.sum(wide * wide, axis=1, keepdims=True)))
    grad_keys, grad_values = grad_keys.astype(BF16), grad_values.astype(BF16)
    result[:tokens, :HD] = grad_keys
    result[:tokens, HD:] = grad_values
    result[tokens:, :] = extra
    stores = [
        pltpu.make_async_copy(result, out.at[copy], out_sems.at[copy])
        for copy in range(out.shape[0])
    ]
    for store in stores:
        store.start()
    for store in stores:
        store.wait()


def gather_kernel(order, grad_kv, own, near, far, rows, gain, *outs):
    shares, (norm_out, total_out, inverse_out) = outs[:4], outs[4:]
    tokens, width = rows.shape
    half = width // 2
    sums = jnp.zeros((EXTRA, tokens), F32)
    for block in range(grad_kv.shape[0]):
        sums = sums + grad_kv[block, tokens:, :].astype(F32)
    inverse = to_column(1.0 / jnp.sqrt(jnp.sum(sums, axis=0, keepdims=True) * (1.0 / D) + EPSILON))
    inverse_out[...] = inverse
    for place, share in enumerate(shares):
        for part in range(2):
            span = slice(part * 2 * HD, (part + 1) * 2 * HD)
            share[:, span] = grad_kv[order[2 * place + part], :tokens, :]
    total_out[...] = (
        nn(shares[0][...], own[...]) + nn(shares[1][...], near[...]) + nn(shares[2][...], far[...])
    )
    norm_out[...] = (rows[...].astype(F32) * inverse * gain[...]).astype(BF16)


def project_kernel(part, share, piece, rows, gain, inverse, scaled_out, prods, gains_out):
    total = part[...] + nn(share[...], piece[...])
    unit = rows[...].astype(F32) * inverse[...]
    scaled = total * gain[...]
    scaled_out[...] = scaled
    gains_out[...] = jnp.sum(total * unit, axis=0, keepdims=True)
    sums = to_row(jnp.sum(scaled * unit, axis=1, keepdims=True))
    for copy in range(prods.shape[0]):
        prods[copy] = sums


def contrib_kernel(prods, scaled, rows, inverse, out):
    mean = to_column(jnp.sum(prods[...], axis=0) * (1.0 / D))
    scale = inverse[...]
    unit = rows[...].astype(F32) * scale
    out[...] = ((scaled[...] - unit * mean) * scale).astype(BF16)


def term_kernel(scale, *refs):
    shares, norms, out = refs[:4], refs[4:8], refs[8]
    total = None
    for share, norm in zip(shares, norms):
        term = (tn(share[...], norm[...]) * scale).astype(BF16).astype(F32)
        total = term if total is None else total + term
    out[...] = total.astype(BF16)


def suffix_kernel(parts, above, out):
    total = above[...].astype(F32)
    for part in reversed(range(parts.shape[0])):
        total = total + parts[part].astype(F32)
        out[part] = total.astype(BF16)


def copy_kernel(source, out):
    out[...] = source[...]


def swap(value, axis, distance):
    count = lax.axis_size(axis)
    return lax.ppermute(value, axis, [(source, source ^ distance) for source in range(count)])


def body(
    inputs,
    norm_gain,
    queries,
    saved_keys,
    saved_values,
    attn_out_grad,
    kv_projection,
    top_grad,
    doc_lengths,
):
    tensor, sections, dp = lax.axis_size("tensor"), lax.axis_size("pipe"), lax.axis_size("dp")
    rows = inputs[0, 0]
    tokens, width = rows.shape
    mine, stage = lax.axis_index("dp"), lax.axis_index("pipe")

    own = kv_projection[0]
    far = swap(own, "dp", 2)

    copies = pl.pallas_call(
        attention_kernel,
        out_shape=jax.ShapeDtypeStruct((tensor, tokens + EXTRA, 2 * HD), BF16),
        in_specs=[SMEM] + [ANY] * 5,
        out_specs=ANY,
        scratch_shapes=[
            pltpu.VMEM((tokens, GROUP * HD), BF16),
            pltpu.VMEM((tokens, HD), BF16),
            pltpu.VMEM((tokens, HD), BF16),
            pltpu.VMEM((tokens, GROUP * HD), BF16),
            pltpu.VMEM((tokens, width), BF16),
            pltpu.VMEM((tokens + EXTRA, 2 * HD), BF16),
            pltpu.SemaphoreType.DMA((3 + GROUP,)),
            pltpu.SemaphoreType.DMA((tensor,)),
        ],
        compiler_params=WHOLE,
        cost_estimate=pl.CostEstimate(flops=int(3e+10), bytes_accessed=4000000, transcendentals=0),
    )(doc_lengths, queries[0, 0], saved_keys[0, 0], saved_values[0, 0], attn_out_grad[0, 0], rows)
    copies, whole = lax.optimization_barrier((copies, own))
    grad_kv = lax.all_to_all(copies, "tensor", 0, 0)
    near = swap(whole, "dp", 1)
    far_near = swap(far, "dp", 1)
    order = [2 * (mine ^ place) + part for place in range(dp) for part in range(2)]

    wide = jax.ShapeDtypeStruct((tokens, width), F32)
    share_shape = jax.ShapeDtypeStruct((tokens, tensor // dp * 2 * HD), BF16)
    *shares, norm, total, inverse = pl.pallas_call(
        gather_kernel,
        out_shape=(share_shape,) * dp
        + (
            jax.ShapeDtypeStruct((tokens, width), BF16),
            wide,
            jax.ShapeDtypeStruct((tokens, 1), F32),
        ),
        in_specs=[SMEM] + [VMEM] * 6,
        out_specs=(VMEM,) * (dp + 3),
        compiler_params=PARAMS,
        cost_estimate=pl.CostEstimate(flops=int(3e10), bytes_accessed=0, transcendentals=0),
    )(jnp.stack(order).astype(jnp.int32), grad_kv, own, near, far, rows, norm_gain)
    scaled, prods, gains = pl.pallas_call(
        project_kernel,
        out_shape=(
            wide,
            jax.ShapeDtypeStruct((tensor, 1, tokens), F32),
            jax.ShapeDtypeStruct((1, width), F32),
        ),
        in_specs=[VMEM] * 6,
        out_specs=(VMEM,) * 3,
        compiler_params=PARAMS,
    )(total, shares[3], far_near, rows, norm_gain, inverse)
    prods = lax.all_to_all(prods, "tensor", 0, 0)

    far_norm, far_share = swap(norm, "dp", 2), swap(shares[2], "dp", 2)

    def local(kernel, shape, *operands):
        return pl.pallas_call(
            kernel,
            out_shape=jax.ShapeDtypeStruct(shape, BF16),
            in_specs=[VMEM] * len(operands),
            out_specs=VMEM,
            compiler_params=SMALL,
        )(*operands)

    contrib = local(contrib_kernel, (tokens, width), prods, scaled, rows, inverse)
    small = tokens // sections
    own_top = lax.dynamic_slice_in_dim(top_grad[0], stage * small, small, 0)
    parts = lax.all_to_all(contrib.reshape(sections, small, width), "pipe", 0, 0)
    parts, far_norm, far_share, gains = lax.optimization_barrier((parts, far_norm, far_share, gains))
    norms = [norm, swap(norm, "dp", 1), far_norm, swap(far_norm, "dp", 1)]
    shares = [shares[0], swap(shares[1], "dp", 1), far_share, swap(shares[3], "dp", 3)]
    suffixes = local(suffix_kernel, parts.shape, parts, own_top)
    section_grads = lax.all_to_all(suffixes, "pipe", 0, 0).reshape(tokens, width)
    section_grads = local(copy_kernel, (tokens, width), section_grads)
    scale = (dp * tokens) ** (-0.5)
    kv_grad = pl.pallas_call(
        functools.partial(term_kernel, scale),
        out_shape=jax.ShapeDtypeStruct((tensor // dp * 2 * HD, width), BF16),
        in_specs=[VMEM] * (2 * dp),
        out_specs=VMEM,
        compiler_params=SMALL,
    )(*shares, *norms)
    gain_grad = lax.psum(gains * scale, "dp")

    return (section_grads[None, None], kv_grad[None], gain_grad)


def solution(mesh):
    placed = (
        P("pipe", "dp", None, "tensor"),
        P("pipe", "tensor"),
        P("pipe", "dp", None, "tensor"),
        P("pipe", "dp", None, "tensor"),
        P("pipe", "dp", None, "tensor"),
        P("pipe", "dp", None, "tensor"),
        P("pipe", "dp", "tensor"),
        P("dp", None, "tensor"),
        P("dp", None),
    )
    return jax.shard_map(
        body,
        mesh=mesh,
        in_specs=placed,
        out_specs=(P("pipe", "dp", None, "tensor"), P("pipe", "dp", "tensor"), P("pipe", "tensor")),
        check_vma=False,
    )
```

```python
import functools

import jax
import jax.numpy as jnp
from jax import lax
from jax.experimental import pallas as pl
from jax.experimental.pallas import tpu as pltpu
from jax.sharding import PartitionSpec as P

D = 8192
H = 64
KVH = 8
HD = 128
GROUP = H // KVH
EPSILON = 1e-05
LOG2E = 1.4426950408889634
F32 = jnp.float32
BF16 = jnp.bfloat16
VMEM = pl.BlockSpec(memory_space=pltpu.VMEM)
SMEM = pl.BlockSpec(memory_space=pltpu.SMEM)
ANY = pl.BlockSpec(memory_space=pl.ANY)
MIB = 1024 * 1024
PARAMS = pltpu.CompilerParams(vmem_limit_bytes=20 * MIB)
SMALL = pltpu.CompilerParams(vmem_limit_bytes=12 * MIB)
WHOLE = pltpu.CompilerParams(vmem_limit_bytes=60 * MIB)


def nt(a, b):
    return lax.dot_general(a, b, (((1,), (1,)), ((), ())), preferred_element_type=F32)


def tn(a, b):
    return lax.dot_general(a, b, (((0,), (0,)), ((), ())), preferred_element_type=F32)


def nn(a, b):
    return jnp.dot(a, b, preferred_element_type=F32)


def to_row(column):
    size = column.shape[0]
    across = lax.broadcasted_iota(jnp.int32, (size, size), 0)
    down = lax.broadcasted_iota(jnp.int32, (size, size), 1)
    return jnp.sum(jnp.where(across == down, column, 0.0), axis=0, keepdims=True)


def to_column(row):
    size = row.shape[1]
    across = lax.broadcasted_iota(jnp.int32, (size, size), 0)
    down = lax.broadcasted_iota(jnp.int32, (size, size), 1)
    return jnp.sum(jnp.where(across == down, row, 0.0), axis=1, keepdims=True)


def attention_kernel(lengths, query, key, value, out_grad, out, *scratch):
    query_v, key_v, value_v, grad_v, result, sems, out_sems = scratch
    tokens = query.shape[0]
    loads = [pltpu.make_async_copy(key, key_v, sems.at[0]), pltpu.make_async_copy(value, value_v, sems.at[1])]
    step = 2 * HD
    for part in range(GROUP // 2):
        span = pl.ds(part * step, step)
        loads.append(pltpu.make_async_copy(query.at[:, span], query_v.at[:, span], sems.at[2 + 2 * part]))
        loads.append(pltpu.make_async_copy(out_grad.at[:, span], grad_v.at[:, span], sems.at[3 + 2 * part]))
    for load in loads:
        load.start()
    key_place = lax.broadcasted_iota(jnp.int32, (tokens, tokens), 0)
    query_place = lax.broadcasted_iota(jnp.int32, (tokens, tokens), 1)
    allowed = key_place <= query_place
    bound = 0
    for index in range(lengths.shape[1]):
        bound = bound + lengths[0, index]
        allowed &= (key_place >= bound) == (query_place >= bound)
    bias = jnp.where(allowed, 0.0, -1e30)
    factor = HD ** (-0.5)
    loads[0].wait()
    loads[1].wait()
    keys, values = key_v[...], value_v[...]
    grad_keys = jnp.zeros((tokens, HD), F32)
    grad_values = jnp.zeros((tokens, HD), F32)
    for head in range(GROUP):
        if head % 2 == 0:
            loads[2 + head].wait()
            loads[3 + head].wait()
        columns = slice(head * HD, (head + 1) * HD)
        rows, grads = query_v[:, columns], grad_v[:, columns]
        scores = nt(keys, rows) + bias
        top = jnp.max(scores, axis=0, keepdims=True)
        expos = jnp.exp2((scores - top) * (factor * LOG2E))
        probs = expos * (1.0 / jnp.sum(expos, axis=0, keepdims=True))
        grad_values += nn(probs.astype(BF16), grads)
        grad_probs = nt(values, grads)
        centre = jnp.sum(probs * grad_probs, axis=0, keepdims=True)
        grad_scores = (probs * ((grad_probs - centre) * factor)).astype(BF16)
        grad_keys += nn(grad_scores, rows)
    grad_keys, grad_values = grad_keys.astype(BF16), grad_values.astype(BF16)
    result[:, :HD] = grad_keys
    result[:, HD:] = grad_values
    stores = [
        pltpu.make_async_copy(result, out.at[copy], out_sems.at[copy])
        for copy in range(out.shape[0])
    ]
    for store in stores:
        store.start()
    for store in stores:
        store.wait()


def gather_kernel(order, grad_kv, own, near, far, rows, *outs):
    shares, (total_out, squares_out) = outs[:4], outs[4:]
    for place, share in enumerate(shares):
        for part in range(2):
            span = slice(part * 2 * HD, (part + 1) * 2 * HD)
            share[:, span] = grad_kv[order[2 * place + part]]
    wide = rows[...].astype(F32)
    squares_out[...] = to_row(jnp.sum(wide * wide, axis=1, keepdims=True))
    total_out[...] = (
        nn(shares[0][...], own[...]) + nn(shares[1][...], near[...]) + nn(shares[2][...], far[...])
    )


def project_kernel(part, share, piece, rows, gain, squares, total_out, sums_out):
    total = part[...] + nn(share[...], piece[...])
    total_out[...] = total
    prods = to_row(jnp.sum(total * gain[...] * rows[...].astype(F32), axis=1, keepdims=True))
    for copy in range(sums_out.shape[0]):
        sums_out[copy, 0:1, :] = prods
        sums_out[copy, 1:2, :] = squares[...]


def contrib_kernel(sums, total, rows, gain, out, inverse_out):
    sums = jnp.sum(sums[...], axis=0)
    across = 1.0 / jnp.sqrt(sums[1:2, :] * (1.0 / D) + EPSILON)
    mean = to_column(sums[0:1, :] * across * (1.0 / D))
    inverse = to_column(across)
    inverse_out[...] = inverse
    unit = rows[...].astype(F32) * inverse
    out[...] = ((total[...] * gain[...] - unit * mean) * inverse).astype(BF16)


def norm_kernel(rows, gain, inverse, total, out, gains_out):
    unit = rows[...].astype(F32) * inverse[...]
    out[...] = (unit * gain[...]).astype(BF16)
    gains_out[...] = jnp.sum(total[...] * unit, axis=0, keepdims=True)


def term_kernel(scale, *refs):
    shares, norms, out = refs[:4], refs[4:8], refs[8]
    total = None
    for share, norm in zip(shares, norms):
        term = (tn(share[...], norm[...]) * scale).astype(BF16).astype(F32)
        total = term if total is None else total + term
    out[...] = total.astype(BF16)


def suffix_kernel(parts, above, out):
    total = above[...].astype(F32)
    for part in reversed(range(parts.shape[0])):
        total = total + parts[part].astype(F32)
        out[part] = total.astype(BF16)


def copy_kernel(source, out):
    out[...] = source[...]


def swap(value, axis, distance):
    count = lax.axis_size(axis)
    return lax.ppermute(value, axis, [(source, source ^ distance) for source in range(count)])


def body(
    inputs,
    norm_gain,
    queries,
    saved_keys,
    saved_values,
    attn_out_grad,
    kv_projection,
    top_grad,
    doc_lengths,
):
    tensor, sections, dp = lax.axis_size("tensor"), lax.axis_size("pipe"), lax.axis_size("dp")
    rows = inputs[0, 0]
    tokens, width = rows.shape
    mine, stage = lax.axis_index("dp"), lax.axis_index("pipe")

    own = kv_projection[0]
    far = swap(own, "dp", 2)

    copies = pl.pallas_call(
        attention_kernel,
        out_shape=jax.ShapeDtypeStruct((tensor, tokens, 2 * HD), BF16),
        in_specs=[SMEM] + [ANY] * 4,
        out_specs=ANY,
        scratch_shapes=[
            pltpu.VMEM((tokens, GROUP * HD), BF16),
            pltpu.VMEM((tokens, HD), BF16),
            pltpu.VMEM((tokens, HD), BF16),
            pltpu.VMEM((tokens, GROUP * HD), BF16),
            pltpu.VMEM((tokens, 2 * HD), BF16),
            pltpu.SemaphoreType.DMA((2 + GROUP,)),
            pltpu.SemaphoreType.DMA((tensor,)),
        ],
        compiler_params=WHOLE,
        cost_estimate=pl.CostEstimate(flops=int(3e+10), bytes_accessed=4000000, transcendentals=0),
    )(doc_lengths, queries[0, 0], saved_keys[0, 0], saved_values[0, 0], attn_out_grad[0, 0])
    copies, whole = lax.optimization_barrier((copies, own))
    grad_kv = lax.all_to_all(copies, "tensor", 0, 0)
    near = swap(whole, "dp", 1)
    far_near = swap(far, "dp", 1)
    order = [2 * (mine ^ place) + part for place in range(dp) for part in range(2)]

    wide = jax.ShapeDtypeStruct((tokens, width), F32)
    share_shape = jax.ShapeDtypeStruct((tokens, tensor // dp * 2 * HD), BF16)
    *shares, total, squares = pl.pallas_call(
        gather_kernel,
        out_shape=(share_shape,) * dp
        + (wide, jax.ShapeDtypeStruct((1, tokens), F32)),
        in_specs=[SMEM] + [VMEM] * 5,
        out_specs=(VMEM,) * (dp + 2),
        compiler_params=PARAMS,
        cost_estimate=pl.CostEstimate(flops=int(3e10), bytes_accessed=0, transcendentals=0),
    )(jnp.stack(order).astype(jnp.int32), grad_kv, own, near, far, rows)
    total, sums = pl.pallas_call(
        project_kernel,
        out_shape=(wide, jax.ShapeDtypeStruct((tensor, 2, tokens), F32)),
        in_specs=[VMEM] * 6,
        out_specs=(VMEM,) * 2,
        compiler_params=PARAMS,
    )(total, shares[3], far_near, rows, norm_gain, squares)
    sums = lax.all_to_all(sums, "tensor", 0, 0)

    def local(kernel, shape, *operands):
        return pl.pallas_call(
            kernel,
            out_shape=jax.ShapeDtypeStruct(shape, BF16),
            in_specs=[VMEM] * len(operands),
            out_specs=VMEM,
            compiler_params=SMALL,
        )(*operands)

    contrib, inverse = pl.pallas_call(
        contrib_kernel,
        out_shape=(
            jax.ShapeDtypeStruct((tokens, width), BF16),
            jax.ShapeDtypeStruct((tokens, 1), F32),
        ),
        in_specs=[VMEM] * 4,
        out_specs=(VMEM,) * 2,
        compiler_params=SMALL,
    )(sums, total, rows, norm_gain)
    small = tokens // sections
    norm, gains = pl.pallas_call(
        norm_kernel,
        out_shape=(
            jax.ShapeDtypeStruct((tokens, width), BF16),
            jax.ShapeDtypeStruct((1, width), F32),
        ),
        in_specs=[VMEM] * 4,
        out_specs=(VMEM,) * 2,
        compiler_params=SMALL,
    )(rows, norm_gain, inverse, total)
    own_top = lax.dynamic_slice_in_dim(top_grad[0], stage * small, small, 0)
    far_norm, far_share = swap(norm, "dp", 2), swap(shares[2], "dp", 2)
    parts = lax.all_to_all(contrib.reshape(sections, small, width), "pipe", 0, 0)
    parts, far_norm, far_share, gains = lax.optimization_barrier((parts, far_norm, far_share, gains))
    norms = [norm, swap(norm, "dp", 1), far_norm, swap(far_norm, "dp", 1)]
    shares = [shares[0], swap(shares[1], "dp", 1), far_share, swap(shares[3], "dp", 3)]
    suffixes = local(suffix_kernel, parts.shape, parts, own_top)
    section_grads = lax.all_to_all(suffixes, "pipe", 0, 0).reshape(tokens, width)
    section_grads = local(copy_kernel, (tokens, width), section_grads)
    scale = (dp * tokens) ** (-0.5)
    kv_grad = pl.pallas_call(
        functools.partial(term_kernel, scale),
        out_shape=jax.ShapeDtypeStruct((tensor // dp * 2 * HD, width), BF16),
        in_specs=[VMEM] * (2 * dp),
        out_specs=VMEM,
        compiler_params=SMALL,
    )(*shares, *norms)
    gain_grad = lax.psum(gains * scale, "dp")

    return (section_grads[None, None], kv_grad[None], gain_grad)


def solution(mesh):
    placed = (
        P("pipe", "dp", None, "tensor"),
        P("pipe", "tensor"),
        P("pipe", "dp", None, "tensor"),
        P("pipe", "dp", None, "tensor"),
        P("pipe", "dp", None, "tensor"),
        P("pipe", "dp", None, "tensor"),
        P("pipe", "dp", "tensor"),
        P("dp", None, "tensor"),
        P("dp", None),
    )
    return jax.shard_map(
        body,
        mesh=mesh,
        in_specs=placed,
        out_specs=(P("pipe", "dp", None, "tensor"), P("pipe", "dp", "tensor"), P("pipe", "tensor")),
        check_vma=False,
    )
```

```python
import functools

import jax
import jax.numpy as jnp
from jax import lax
from jax.experimental import pallas as pl
from jax.experimental.pallas import tpu as pltpu
from jax.sharding import PartitionSpec as P

D = 8192
H = 64
KVH = 8
HD = 128
GROUP = H // KVH
EPSILON = 1e-05
EXTRA = 16
LOG2E = 1.4426950408889634
F32 = jnp.float32
BF16 = jnp.bfloat16
VMEM = pl.BlockSpec(memory_space=pltpu.VMEM)
SMEM = pl.BlockSpec(memory_space=pltpu.SMEM)
ANY = pl.BlockSpec(memory_space=pl.ANY)
MIB = 1024 * 1024
PARAMS = pltpu.CompilerParams(vmem_limit_bytes=20 * MIB)
SMALL = pltpu.CompilerParams(vmem_limit_bytes=12 * MIB)
WHOLE = pltpu.CompilerParams(vmem_limit_bytes=60 * MIB)


def nt(a, b):
    return lax.dot_general(a, b, (((1,), (1,)), ((), ())), preferred_element_type=F32)


def tn(a, b):
    return lax.dot_general(a, b, (((0,), (0,)), ((), ())), preferred_element_type=F32)


def nn(a, b):
    return jnp.dot(a, b, preferred_element_type=F32)


def to_row(column):
    size = column.shape[0]
    across = lax.broadcasted_iota(jnp.int32, (size, size), 0)
    down = lax.broadcasted_iota(jnp.int32, (size, size), 1)
    return jnp.sum(jnp.where(across == down, column, 0.0), axis=0, keepdims=True)


def to_column(row):
    size = row.shape[1]
    across = lax.broadcasted_iota(jnp.int32, (size, size), 0)
    down = lax.broadcasted_iota(jnp.int32, (size, size), 1)
    return jnp.sum(jnp.where(across == down, row, 0.0), axis=1, keepdims=True)


def in_three_rows(row):
    high = row.astype(BF16).astype(F32)
    middle = (row - high).astype(BF16).astype(F32)
    low = row - high - middle
    place = lax.broadcasted_iota(jnp.int32, (EXTRA, row.shape[1]), 0)
    rows = jnp.where(place == 0, high, jnp.where(place == 1, middle, jnp.where(place == 2, low, 0.0)))
    return rows.astype(BF16)


def attention_kernel(lengths, query, key, value, out_grad, inputs, out, *scratch):
    query_v, key_v, value_v, grad_v, inputs_v, result, sems, out_sems = scratch
    tokens = query.shape[0]
    loads = [pltpu.make_async_copy(key, key_v, sems.at[0]), pltpu.make_async_copy(value, value_v, sems.at[1])]
    step = 2 * HD
    for part in range(GROUP // 2):
        span = pl.ds(part * step, step)
        loads.append(pltpu.make_async_copy(query.at[:, span], query_v.at[:, span], sems.at[2 + 2 * part]))
        loads.append(pltpu.make_async_copy(out_grad.at[:, span], grad_v.at[:, span], sems.at[3 + 2 * part]))
    loads.append(pltpu.make_async_copy(inputs, inputs_v, sems.at[2 + GROUP]))
    for load in loads:
        load.start()
    key_place = lax.broadcasted_iota(jnp.int32, (tokens, tokens), 0)
    query_place = lax.broadcasted_iota(jnp.int32, (tokens, tokens), 1)
    allowed = key_place <= query_place
    bound = 0
    for index in range(lengths.shape[1]):
        bound = bound + lengths[0, index]
        allowed &= (key_place >= bound) == (query_place >= bound)
    bias = jnp.where(allowed, 0.0, -1e30)
    factor = HD ** (-0.5)
    loads[0].wait()
    loads[1].wait()
    keys, values = key_v[...], value_v[...]
    grad_keys = jnp.zeros((tokens, HD), F32)
    grad_values = jnp.zeros((tokens, HD), F32)
    for head in range(GROUP):
        if head % 2 == 0:
            loads[2 + head].wait()
            loads[3 + head].wait()
        columns = slice(head * HD, (head + 1) * HD)
        rows, grads = query_v[:, columns], grad_v[:, columns]
        scores = nt(keys, rows) + bias
        top = jnp.max(scores, axis=0, keepdims=True)
        expos = jnp.exp2((scores - top) * (factor * LOG2E))
        probs = expos * (1.0 / jnp.sum(expos, axis=0, keepdims=True))
        grad_values += nn(probs.astype(BF16), grads)
        grad_probs = nt(values, grads)
        centre = jnp.sum(probs * grad_probs, axis=0, keepdims=True)
        grad_scores = (probs * ((grad_probs - centre) * factor)).astype(BF16)
        grad_keys += nn(grad_scores, rows)
    loads[2 + GROUP].wait()
    wide = inputs_v[...].astype(F32)
    extra = in_three_rows(to_row(jnp.sum(wide * wide, axis=1, keepdims=True)))
    grad_keys, grad_values = grad_keys.astype(BF16), grad_values.astype(BF16)
    result[:tokens, :HD] = grad_keys
    result[:tokens, HD:] = grad_values
    result[tokens:, :] = extra
    stores = [
        pltpu.make_async_copy(result, out.at[copy], out_sems.at[copy])
        for copy in range(out.shape[0])
    ]
    for store in stores:
        store.start()
    for store in stores:
        store.wait()


def gather_kernel(order, grad_kv, own, near, far, *outs):
    shares, (total_out, inverse_out) = outs[:4], outs[4:]
    tokens = total_out.shape[0]
    sums = jnp.zeros((EXTRA, tokens), F32)
    for block in range(grad_kv.shape[0]):
        sums = sums + grad_kv[block, tokens:, :].astype(F32)
    inverse = to_column(1.0 / jnp.sqrt(jnp.sum(sums, axis=0, keepdims=True) * (1.0 / D) + EPSILON))
    inverse_out[...] = inverse
    for place, share in enumerate(shares):
        for part in range(2):
            span = slice(part * 2 * HD, (part + 1) * 2 * HD)
            share[:, span] = grad_kv[order[2 * place + part], :tokens, :]
    total_out[...] = (
        nn(shares[0][...], own[...]) + nn(shares[1][...], near[...]) + nn(shares[2][...], far[...])
    )


def norm_kernel(rows, gain, inverse, out):
    out[...] = (rows[...].astype(F32) * inverse[...] * gain[...]).astype(BF16)


def project_kernel(part, share, piece, rows, gain, inverse, scaled_out, prods, gains_out):
    total = part[...] + nn(share[...], piece[...])
    unit = rows[...].astype(F32) * inverse[...]
    scaled = total * gain[...]
    scaled_out[...] = scaled
    gains_out[...] = jnp.sum(total * unit, axis=0, keepdims=True)
    sums = to_row(jnp.sum(scaled * unit, axis=1, keepdims=True))
    for copy in range(prods.shape[0]):
        prods[copy] = sums


def contrib_kernel(prods, scaled, rows, inverse, out):
    mean = to_column(jnp.sum(prods[...], axis=0) * (1.0 / D))
    scale = inverse[...]
    unit = rows[...].astype(F32) * scale
    out[...] = ((scaled[...] - unit * mean) * scale).astype(BF16)


def term_kernel(scale, *refs):
    shares, norms, out = refs[:4], refs[4:8], refs[8]
    total = None
    for share, norm in zip(shares, norms):
        term = (tn(share[...], norm[...]) * scale).astype(BF16).astype(F32)
        total = term if total is None else total + term
    out[...] = total.astype(BF16)


def suffix_kernel(parts, above, out):
    total = above[...].astype(F32)
    for part in reversed(range(parts.shape[0])):
        total = total + parts[part].astype(F32)
        out[part] = total.astype(BF16)


def copy_kernel(source, out):
    out[...] = source[...]


def swap(value, axis, distance):
    count = lax.axis_size(axis)
    return lax.ppermute(value, axis, [(source, source ^ distance) for source in range(count)])


def body(
    inputs,
    norm_gain,
    queries,
    saved_keys,
    saved_values,
    attn_out_grad,
    kv_projection,
    top_grad,
    doc_lengths,
):
    tensor, sections, dp = lax.axis_size("tensor"), lax.axis_size("pipe"), lax.axis_size("dp")
    rows = inputs[0, 0]
    tokens, width = rows.shape
    mine, stage = lax.axis_index("dp"), lax.axis_index("pipe")

    own = kv_projection[0]
    far = swap(own, "dp", 2)

    copies = pl.pallas_call(
        attention_kernel,
        out_shape=jax.ShapeDtypeStruct((tensor, tokens + EXTRA, 2 * HD), BF16),
        in_specs=[SMEM] + [ANY] * 5,
        out_specs=ANY,
        scratch_shapes=[
            pltpu.VMEM((tokens, GROUP * HD), BF16),
            pltpu.VMEM((tokens, HD), BF16),
            pltpu.VMEM((tokens, HD), BF16),
            pltpu.VMEM((tokens, GROUP * HD), BF16),
            pltpu.VMEM((tokens, width), BF16),
            pltpu.VMEM((tokens + EXTRA, 2 * HD), BF16),
            pltpu.SemaphoreType.DMA((3 + GROUP,)),
            pltpu.SemaphoreType.DMA((tensor,)),
        ],
        compiler_params=WHOLE,
        cost_estimate=pl.CostEstimate(flops=int(3e+10), bytes_accessed=4000000, transcendentals=0),
    )(doc_lengths, queries[0, 0], saved_keys[0, 0], saved_values[0, 0], attn_out_grad[0, 0], rows)
    copies, whole = lax.optimization_barrier((copies, own))
    grad_kv = lax.all_to_all(copies, "tensor", 0, 0)
    near = swap(whole, "dp", 1)
    far_near = swap(far, "dp", 1)
    order = [2 * (mine ^ place) + part for place in range(dp) for part in range(2)]

    wide = jax.ShapeDtypeStruct((tokens, width), F32)
    share_shape = jax.ShapeDtypeStruct((tokens, tensor // dp * 2 * HD), BF16)
    *shares, total, inverse = pl.pallas_call(
        gather_kernel,
        out_shape=(share_shape,) * dp
        + (wide, jax.ShapeDtypeStruct((tokens, 1), F32)),
        in_specs=[SMEM] + [VMEM] * 4,
        out_specs=(VMEM,) * (dp + 2),
        compiler_params=PARAMS,
        cost_estimate=pl.CostEstimate(flops=int(3e10), bytes_accessed=0, transcendentals=0),
    )(jnp.stack(order).astype(jnp.int32), grad_kv, own, near, far)
    scaled, prods, gains = pl.pallas_call(
        project_kernel,
        out_shape=(
            wide,
            jax.ShapeDtypeStruct((tensor, 1, tokens), F32),
            jax.ShapeDtypeStruct((1, width), F32),
        ),
        in_specs=[VMEM] * 6,
        out_specs=(VMEM,) * 3,
        compiler_params=PARAMS,
    )(total, shares[3], far_near, rows, norm_gain, inverse)
    prods = lax.all_to_all(prods, "tensor", 0, 0)


    def local(kernel, shape, *operands):
        return pl.pallas_call(
            kernel,
            out_shape=jax.ShapeDtypeStruct(shape, BF16),
            in_specs=[VMEM] * len(operands),
            out_specs=VMEM,
            compiler_params=SMALL,
        )(*operands)

    contrib = local(contrib_kernel, (tokens, width), prods, scaled, rows, inverse)
    small = tokens // sections
    own_top = lax.dynamic_slice_in_dim(top_grad[0], stage * small, small, 0)
    contrib, late = lax.optimization_barrier((contrib, inverse))
    norm = local(norm_kernel, (tokens, width), rows, norm_gain, late)
    far_norm, far_share = swap(norm, "dp", 2), swap(shares[2], "dp", 2)
    parts = lax.all_to_all(contrib.reshape(sections, small, width), "pipe", 0, 0)
    parts, far_norm, far_share, gains = lax.optimization_barrier((parts, far_norm, far_share, gains))
    norms = [norm, swap(norm, "dp", 1), far_norm, swap(far_norm, "dp", 1)]
    shares = [shares[0], swap(shares[1], "dp", 1), far_share, swap(shares[3], "dp", 3)]
    suffixes = local(suffix_kernel, parts.shape, parts, own_top)
    section_grads = lax.all_to_all(suffixes, "pipe", 0, 0).reshape(tokens, width)
    section_grads = local(copy_kernel, (tokens, width), section_grads)
    scale = (dp * tokens) ** (-0.5)
    kv_grad = pl.pallas_call(
        functools.partial(term_kernel, scale),
        out_shape=jax.ShapeDtypeStruct((tensor // dp * 2 * HD, width), BF16),
        in_specs=[VMEM] * (2 * dp),
        out_specs=VMEM,
        compiler_params=SMALL,
    )(*shares, *norms)
    gain_grad = lax.psum(gains * scale, "dp")

    return (section_grads[None, None], kv_grad[None], gain_grad)


def solution(mesh):
    placed = (
        P("pipe", "dp", None, "tensor"),
        P("pipe", "tensor"),
        P("pipe", "dp", None, "tensor"),
        P("pipe", "dp", None, "tensor"),
        P("pipe", "dp", None, "tensor"),
        P("pipe", "dp", None, "tensor"),
        P("pipe", "dp", "tensor"),
        P("dp", None, "tensor"),
        P("dp", None),
    )
    return jax.shard_map(
        body,
        mesh=mesh,
        in_specs=placed,
        out_specs=(P("pipe", "dp", None, "tensor"), P("pipe", "dp", "tensor"), P("pipe", "tensor")),
        check_vma=False,
    )
```
